32 devices in a mesh: groups: 1, ctx: 32 (over z, y, x, core).
Axes of the slice: x: 2, y: 2, z: 4, core: 2. Of those that a mesh axis runs over, the one named last changes fastest.
Arguments:
- queries: bfloat16 [4096, 2048], P(('groups', 'ctx')), may hold values from -120 to 120
- self_keys: bfloat16 [4096, 2048], P(('groups', 'ctx')), may hold values from -6 to 6
- self_values: bfloat16 [4096, 2048], P(('groups', 'ctx')), may hold values from -6 to 6
- cross_queries: bfloat16 [4096, 2048], P(('groups', 'ctx')), may hold values from -6 to 6
- encoded: bfloat16 [4096, 896], P(('groups', 'ctx')), may hold values from -6 to 6
- neighbour_weight: bfloat16 [896, 4096], replicated, may hold values from -1 to 1
- counts: int32 [64], P(('groups', 'ctx')), may hold values from 0 to 2
- sources: int32 [64, 2], P(('groups', 'ctx')), may hold values from 0 to 61, as said below
Outputs:
- attended: bfloat16 [4096, 2048], P(('groups', 'ctx'))
The draws below stay inside these ranges and needn't reach their ends.
Inputs may be any that keep to these rules, and one draw needn't show every extreme that they name: sources[c, j] equals max(c - 1 - r, 0) for some r with 1 <= r <= 29.
All inputs are finite; a program needn't handle non-finite values.
Results may differ from the reference program's by a relative error of at most 0.0061.
Values may be sent and summed in bfloat16 or wider, within the bound.
A program may use at most 128 MiB of HBM per device.

```python
import jax
import jax.numpy as jnp
from jax import lax

HEADS = 16
HEAD_DIM = 128
WIDTH = 2048
ENC = 896
SPAN = 64
WINDOW = 2048
CH_DEV = 2
TOK_DEV = 128
REACH = 16
TOKENS = 4096
SPANS = 64


def paired_rows(key):
    key_rows = jax.random.truncated_normal(jax.random.fold_in(key, 11), -6.0, 6.0, (TOKENS, WIDTH), jnp.float32)
    query_rows = jax.random.truncated_normal(jax.random.fold_in(key, 12), -6.0, 6.0, (TOKENS, WIDTH), jnp.float32)
    return (key_rows, query_rows)


def draw_queries(key, part):
    key_rows, query_rows = paired_rows(key)
    return query_rows.astype(jnp.bfloat16)


def draw_self_keys(key, part):
    key_rows, query_rows = paired_rows(key)
    return key_rows.astype(jnp.bfloat16)


def draw_neighbour_weight(key, part):
    base = jax.random.truncated_normal(jax.random.fold_in(key, 41), -4.0, 4.0, (ENC, 2 * WIDTH), jnp.float32) * ENC ** (-0.5)
    return base.astype(jnp.bfloat16)


def draw_encoded(key, part):
    rows = jax.random.truncated_normal(jax.random.fold_in(key, 21), -6.0, 6.0, (TOKENS, ENC), jnp.float32)
    return rows.astype(jnp.bfloat16)


def draw_cross_queries(key, part):
    rows = jax.random.truncated_normal(jax.random.fold_in(key, 31), -6.0, 6.0, (TOKENS, WIDTH), jnp.float32)
    return rows.astype(jnp.bfloat16)


def draw_sources(key, part):
    span_ids = jnp.arange(SPANS, dtype=jnp.int32)[:, None]
    backward = jax.random.randint(key, (SPANS, 2), 1, (REACH - 1) * CH_DEV, dtype=jnp.int32)
    row_ids = jnp.arange(SPANS, dtype=jnp.int32)[:, None]
    slot_ids = jnp.arange(2, dtype=jnp.int32)[None, :]
    nearest = (row_ids == SPANS - 1) & (slot_ids == 0)
    backward = jnp.where(nearest, 1, backward)
    return jnp.maximum(span_ids - 1 - backward, 0)


def touch_ends(drawn, rng, least, high):
    longest = drawn.shape.index(max(drawn.shape))
    spots = []
    for shift in (0, 1):
        where = [jax.random.randint(jax.random.fold_in(rng, axis), (), 0, length) for axis, length in enumerate(drawn.shape)]
        where[longest] = (where[longest] + shift) % drawn.shape[longest]
        spots.append(tuple(where))
    return drawn.at[spots[0]].set(least).at[spots[1]].set(high)


def shard_levels(stream_key, shape, cuts, smallest, top_value):
    factor_of, own = 1.0, jax.random.fold_in(stream_key, 6)
    for dim, parts in cuts:
        draws = jnp.exp(jax.random.uniform(jax.random.fold_in(own, dim), (parts,), jnp.float32, smallest / len(cuts), top_value / len(cuts)))
        factor_of = factor_of * jnp.repeat(draws, shape[dim] // parts).reshape([-1 if axis == dim else 1 for axis in range(len(shape))])
    return factor_of


def centred(stream_key, dims, scale, reach, cuts=(), held_as=jnp.bfloat16):
    loudness = shard_levels(stream_key, dims, cuts, -0.22, 0.18) if cuts else 1.0
    result = jax.random.normal(stream_key, dims, jnp.float32) * scale * loudness
    return jnp.minimum(jnp.maximum(result, -reach), reach).astype(held_as)


def setup_inputs(seed: int = 0, part: int = 0) -> dict:
    arg_keys = jax.random.split(jax.random.key(seed), 9)
    part_splits = jax.random.split(jax.random.fold_in(arg_keys[8], part), 9)
    queries = draw_queries(jax.random.fold_in(jax.random.fold_in(arg_keys[8], part), 71), part)
    self_keys = draw_self_keys(jax.random.fold_in(jax.random.fold_in(arg_keys[8], part), 71), part)
    self_values = centred(part_splits[2], (TOKENS, WIDTH), 1.0, 6.0, ((0, 32),))
    cross_queries = draw_cross_queries(jax.random.fold_in(jax.random.fold_in(arg_keys[8], part), 71), part)
    encoded = draw_encoded(jax.random.fold_in(jax.random.fold_in(arg_keys[8], part), 71), part)
    neighbour_weight = draw_neighbour_weight(jax.random.fold_in(arg_keys[8], 71), part)
    counts = touch_ends(jax.random.randint(part_splits[6], (SPANS,), 0, 3), jax.random.fold_in(part_splits[6], 1), 0, 2).astype(jnp.int32)
    sources = draw_sources(jax.random.fold_in(jax.random.fold_in(arg_keys[8], part), 71), part)
    return {"queries": queries, "self_keys": self_keys, "self_values": self_values, "cross_queries": cross_queries, "encoded": encoded, "neighbour_weight": neighbour_weight, "counts": counts, "sources": sources}


MASKED_SCORE = -1.0e30


def masked_weights(scores, valid_mask, extra_total):
    masked = jnp.where(valid_mask, scores, MASKED_SCORE)
    largest = jnp.max(masked, axis=-1, keepdims=True)
    exponent = jnp.where(valid_mask, jnp.exp(masked - largest), 0.0)
    totals = jnp.sum(exponent, axis=-1, keepdims=True)
    return (exponent / (totals + extra_total)).astype(jnp.bfloat16)


def reference(queries, self_keys, self_values, cross_queries, encoded, neighbour_weight, counts, sources):
    scale_factor = HEAD_DIM ** -0.5
    padding = jnp.zeros((WINDOW, WIDTH), jnp.bfloat16)
    keys_padded = jnp.concatenate([padding, self_keys], axis=0)
    values_padded = jnp.concatenate([padding, self_values], axis=0)
    query_index = jnp.arange(TOK_DEV, dtype=jnp.int32)[:, None]
    key_index = jnp.arange(WINDOW + TOK_DEV, dtype=jnp.int32)[None, :]

    def self_block(block_index):
        block_start = (block_index * TOK_DEV).astype(jnp.int32)
        query_block = lax.dynamic_slice_in_dim(queries, block_start, TOK_DEV, 0).reshape(TOK_DEV, HEADS, HEAD_DIM).astype(jnp.float32)
        key_block = lax.dynamic_slice_in_dim(keys_padded, block_start, WINDOW + TOK_DEV, 0).reshape(WINDOW + TOK_DEV, HEADS, HEAD_DIM).astype(jnp.float32)
        value_block = lax.dynamic_slice_in_dim(values_padded, block_start, WINDOW + TOK_DEV, 0).reshape(WINDOW + TOK_DEV, HEADS, HEAD_DIM).astype(jnp.float32)
        scores = jnp.einsum("rhd,ihd->hri", query_block, key_block) * scale_factor
        valid_mask = (key_index > query_index) & (key_index <= query_index + WINDOW) & (key_index >= WINDOW - block_start)
        weights = masked_weights(scores, valid_mask[None], 0.0)
        weights = lax.optimization_barrier(weights).astype(jnp.float32)
        return jnp.einsum("hri,ihd->rhd", weights, value_block).reshape(TOK_DEV, WIDTH)

    self_part = lax.map(self_block, jnp.arange(TOKENS // TOK_DEV, dtype=jnp.int32)).reshape(TOKENS, WIDTH)

    projected = jnp.dot(encoded, neighbour_weight, preferred_element_type=jnp.float32).astype(jnp.bfloat16)
    slot_index = jnp.arange(4 * SPAN, dtype=jnp.int32) // (2 * SPAN)

    def cross_span(span_index):
        previous = jnp.maximum(span_index - 1, 0).astype(jnp.int32)
        neighbour_count = jnp.where(span_index > 0, counts[previous], 0)
        span_sources = sources[previous]
        pieces = [lax.dynamic_slice_in_dim(projected, (span_sources[slot] * SPAN).astype(jnp.int32), 2 * SPAN, 0) for slot in range(2)]
        neighbour_rows = jnp.concatenate(pieces, axis=0)
        neighbour_keys = neighbour_rows[:, :WIDTH].reshape(4 * SPAN, HEADS, HEAD_DIM).astype(jnp.float32)
        neighbour_values = neighbour_rows[:, WIDTH:].reshape(4 * SPAN, HEADS, HEAD_DIM).astype(jnp.float32)
        query_block = lax.dynamic_slice_in_dim(cross_queries, (span_index * SPAN).astype(jnp.int32), SPAN, 0).reshape(SPAN, HEADS, HEAD_DIM).astype(jnp.float32)
        scores = jnp.einsum("qhd,khd->hqk", query_block, neighbour_keys) * scale_factor
        valid_mask = (slot_index < neighbour_count)[None, None, :]
        extra_total = jnp.where(neighbour_count > 0, 0.0, 1.0)
        weights = masked_weights(scores, valid_mask, extra_total)
        weights = lax.optimization_barrier(weights).astype(jnp.float32)
        return jnp.einsum("hqk,khd->qhd", weights, neighbour_values).reshape(SPAN, WIDTH)

    cross_part = lax.map(cross_span, jnp.arange(SPANS, dtype=jnp.int32)).reshape(TOKENS, WIDTH)
    return (self_part + cross_part).astype(jnp.bfloat16)
```

```python
import functools

import jax
import jax.numpy as jnp
from jax import lax
from jax.experimental import pallas as pl
from jax.experimental.pallas import tpu as pltpu
from jax.sharding import PartitionSpec as P

HEAD_DIM = 128
SPAN = 64
REACH = 16
MASKED_SCORE = -1e30
LOG2E = 1.4426950408889634

ENC, Q_OWN, K_OWN, V_OWN, K_PREV, V_PREV, CQ, META, META_PREV = range(9)
PK_OWN, PV_OWN, PK_PREV, PV_PREV, OUT, KINDS = range(9, 15)
LOCAL_W, LOCAL_E, LOCAL_META, LOCALS = range(4)


def dot_t(a, b):
    return lax.dot_general(a, b, (((1,), (1,)), ((), ())), preferred_element_type=jnp.float32)


def kernel(
    group,
    chunks,
    span_count,
    q_in,
    k_in,
    v_in,
    cq_in,
    e_in,
    w_in,
    meta_in,
    out,
    qs,
    ks,
    vs,
    cqs,
    meta_v,
    meta_s,
    enc_own,
    enc_prev,
    weight,
    proj_own,
    proj_prev,
    pks,
    pvs,
    self_out,
    stage,
    send,
    recv,
    local,
):
    tok = q_in.shape[0]
    width = q_in.shape[1]
    window = group * tok
    me = lax.axis_index("ctx")
    chunk = lax.div(me, group)
    off = lax.rem(me, group)
    scale = LOG2E * HEAD_DIM ** (-0.5)
    has_prev = chunk > 0
    has_next = chunk < chunks - 1

    def own_peer(step):
        return lax.rem(off + step, group)

    def columns(index):
        return pl.ds(pl.multiple_of(index * HEAD_DIM, HEAD_DIM), HEAD_DIM)

    def rows(index, base=0):
        return pl.ds(pl.multiple_of(base + index * tok, tok), tok)

    def remote(src, dst, kind, device):
        pltpu.make_async_remote_copy(
            src_ref=src,
            dst_ref=dst,
            send_sem=send.at[kind],
            recv_sem=recv.at[kind],
            device_id={"ctx": device},
            device_id_type=pl.DeviceIdType.MESH,
        ).start()

    def arrived(region, kind):
        pltpu.make_async_copy(region, region, recv.at[kind]).wait()

    def sent(region, kind):
        pltpu.make_async_copy(region, region, send.at[kind]).wait()

    load_w = pltpu.make_async_copy(w_in, weight, local.at[LOCAL_W])
    load_e = pltpu.make_async_copy(e_in, enc_own, local.at[LOCAL_E])
    load_e.start()
    load_w.start()

    barrier = pltpu.get_barrier_semaphore()

    def greet(device):
        pl.semaphore_signal(
            barrier, inc=1, device_id={"ctx": device}, device_id_type=pl.DeviceIdType.MESH
        )

    @pl.loop(1, group)
    def _(step):
        greet(chunk * group + own_peer(step))

    @pl.when(has_prev)
    def _():
        @pl.loop(0, group)
        def _(step):
            greet((chunk - 1) * group + own_peer(step))

    @pl.when(has_next)
    def _():
        @pl.loop(0, group)
        def _(step):
            greet((chunk + 1) * group + own_peer(step))

    friends = group - 1 + jnp.where(has_prev, group, 0) + jnp.where(has_next, group, 0)
    pl.semaphore_wait(barrier, friends)

    @pl.when(has_next)
    def _():
        remote(e_in, enc_prev, ENC, (chunk + 1) * group + off)

    @pl.loop(0, group)
    def _(step):
        peer = own_peer(step)
        cols = columns(peer)

        @pl.when(has_next)
        def _():
            target = (chunk + 1) * group + peer
            remote(k_in.at[:, cols], ks.at[rows(off)], K_PREV, target)
            remote(v_in.at[:, cols], vs.at[rows(off)], V_PREV, target)

        @pl.when(step > 0)
        def _():
            target = chunk * group + peer
            remote(k_in.at[:, cols], ks.at[rows(off, window)], K_OWN, target)
            remote(v_in.at[:, cols], vs.at[rows(off, window)], V_OWN, target)
            remote(q_in.at[:, cols], qs.at[rows(off)], Q_OWN, target)

    def own_copy(src, dst, kind):
        pltpu.make_async_copy(src, dst, recv.at[kind]).start()

    mine = columns(off)
    own_copy(k_in.at[:, mine], ks.at[rows(off, window)], K_OWN)
    own_copy(v_in.at[:, mine], vs.at[rows(off, window)], V_OWN)
    own_copy(q_in.at[:, mine], qs.at[rows(off)], Q_OWN)
    own_copy(cq_in.at[:, mine], cqs.at[rows(off)], CQ)
    own_meta = pl.ds(pl.multiple_of(8 * (off + 1), 8), 8)
    own_copy(meta_in, meta_v.at[own_meta], META)

    @pl.when(has_next & (off == group - 1))
    def _():
        @pl.loop(0, group)
        def _(step):
            remote(meta_in, meta_v.at[pl.ds(0, 8)], META_PREV, (chunk + 1) * group + own_peer(step))

    @pl.loop(1, group)
    def _(step):
        peer = own_peer(step)
        target = chunk * group + peer
        remote(cq_in.at[:, columns(peer)], cqs.at[rows(off)], CQ, target)
        remote(meta_in, meta_v.at[own_meta], META, target)

    load_w.wait()
    load_e.wait()

    def project(encoded, proj, base, key_kind, value_kind):
        @pl.loop(0, group // 2)
        def _(step):
            pair = lax.rem(lax.div(off, 2) + step, group // 2)
            for part, (dst, kind) in enumerate(((pks, key_kind), (pvs, value_kind))):
                start = pl.multiple_of(part * width + pair * 2 * HEAD_DIM, 2 * HEAD_DIM)
                both = pl.ds(start, 2 * HEAD_DIM)
                proj[:, both] = jnp.dot(
                    encoded[...], weight[:, both], preferred_element_type=jnp.float32
                ).astype(jnp.bfloat16)
                for half in range(2):
                    peer = pair * 2 + half
                    cols = pl.ds(pl.multiple_of(part * width + peer * HEAD_DIM, HEAD_DIM), HEAD_DIM)

                    @pl.when(peer != off)
                    def _():
                        remote(proj.at[:, cols], dst.at[rows(off, base)], kind, chunk * group + peer)

                    @pl.when(peer == off)
                    def _():
                        own_copy(proj.at[:, cols], dst.at[rows(off, base)], kind)

    project(enc_own, proj_own, window, PK_OWN, PV_OWN)

    @pl.when(has_prev)
    def _():
        arrived(enc_prev, ENC)
        project(enc_prev, proj_prev, 0, PK_PREV, PV_PREV)

    first_half = pl.ds(0, window)
    second_half = pl.ds(window, window)

    @pl.when(jnp.logical_not(has_prev))
    def _():
        ks[first_half, :] = jnp.zeros((window, HEAD_DIM), jnp.bfloat16)
        vs[first_half, :] = jnp.zeros((window, HEAD_DIM), jnp.bfloat16)
        pks[first_half, :] = jnp.zeros((window, HEAD_DIM), jnp.bfloat16)
        pvs[first_half, :] = jnp.zeros((window, HEAD_DIM), jnp.bfloat16)
        meta_v[pl.ds(0, 8), :] = jnp.zeros((8, meta_v.shape[1]), jnp.int32)

    arrived(qs, Q_OWN)
    arrived(ks.at[second_half], K_OWN)
    arrived(vs.at[second_half], V_OWN)

    @pl.when(has_prev)
    def _():
        arrived(ks.at[first_half], K_PREV)
        arrived(vs.at[first_half], V_PREV)

    tile = 2 * tok
    reach = window + tile

    @pl.loop(0, window // tile)
    def _(index):
        start = pl.multiple_of(index * tile, tile)
        queries = qs[pl.ds(start, tile), :]
        keys = ks[pl.ds(start, reach), :]
        values = vs[pl.ds(start, reach), :]
        least = jnp.where(has_prev, 0, window - start)
        scores = dot_t(queries, keys)
        row = lax.broadcasted_iota(jnp.int32, (tile, tile), 0)
        col = lax.broadcasted_iota(jnp.int32, (tile, tile), 1)
        mid = lax.broadcasted_iota(jnp.int32, (1, window - tile), 1) + tile
        head = jnp.where((col > row) & (col >= least), scores[:, :tile], MASKED_SCORE)
        body = jnp.where(mid >= least, scores[:, tile:window], MASKED_SCORE)
        tail = jnp.where(col <= row, scores[:, window:], MASKED_SCORE)
        scores = jnp.concatenate([head, body, tail], axis=1)
        largest = jnp.max(scores, axis=-1, keepdims=True)
        exponent = jnp.exp2((scores - largest) * scale)
        total = jnp.sum(exponent, axis=-1, keepdims=True)
        result = jnp.dot(exponent.astype(jnp.bfloat16), values, preferred_element_type=jnp.float32)
        self_out[pl.ds(start, tile), :] = result / total

    arrived(meta_v.at[pl.ds(8, 8 * group)], META)
    arrived(cqs, CQ)
    arrived(pks.at[second_half], PK_OWN)
    arrived(pvs.at[second_half], PV_OWN)

    @pl.when(has_prev)
    def _():
        arrived(meta_v.at[pl.ds(0, 8)], META_PREV)
        arrived(pks.at[first_half], PK_PREV)
        arrived(pvs.at[first_half], PV_PREV)

    to_scalar = pltpu.make_async_copy(meta_v, meta_s, local.at[LOCAL_META])
    to_scalar.start()
    to_scalar.wait()

    @pl.loop(0, window // tile)
    def _(index):
        start = pl.multiple_of(index * tile, tile)
        lowest = pl.multiple_of(start + SPAN, SPAN)
        across = window + tile - 2 * SPAN
        keys = pks[pl.ds(lowest, across), :]
        values = pvs[pl.ds(lowest, across), :]
        scores = dot_t(cqs[pl.ds(start, tile), :], keys)
        place = lax.broadcasted_iota(jnp.int32, (1, across), 1) + lowest
        parts, totals = [], []
        for piece in range(tile // SPAN):
            span = index * (tile // SPAN) + piece
            entry = span + span_count - 1
            block = lax.div(entry, span_count) * 8
            lane = lax.rem(entry, span_count) * 3
            real = has_prev | (span > 0)
            count = jnp.where(real, meta_s[block, lane], 0)
            times = jnp.zeros((1, across), jnp.float32)
            for slot in range(2):
                first = meta_s[block, lane + 1 + slot] * SPAN - (chunk - 1) * window
                first = jnp.where(slot < count, first, -4 * window)
                inside = (place >= first) & (place < first + 2 * SPAN)
                times = times + jnp.where(inside, 1.0, 0.0)
            piece_scores = scores[piece * SPAN : (piece + 1) * SPAN]
            piece_scores = jnp.where(times > 0.0, piece_scores, MASKED_SCORE)
            largest = jnp.max(piece_scores, axis=-1, keepdims=True)
            exponent = jnp.exp2((piece_scores - largest) * scale) * times
            total = jnp.sum(exponent, axis=-1, keepdims=True)
            totals.append(total + jnp.where(count > 0, 0.0, 1.0))
            parts.append(exponent.astype(jnp.bfloat16))
        result = jnp.dot(
            jnp.concatenate(parts, axis=0), values, preferred_element_type=jnp.float32
        ) / jnp.concatenate(totals, axis=0)
        both = self_out[pl.ds(start, tile), :] + result
        stage[pl.ds(start, tile), :] = both.astype(jnp.bfloat16)
        for half in range(tile // tok):
            owner = index * (tile // tok) + half

            @pl.when(owner != off)
            def _():
                remote(stage.at[rows(owner)], out.at[:, mine], OUT, chunk * group + owner)

            @pl.when(owner == off)
            def _():
                own_copy(stage.at[rows(owner)], out.at[:, mine], OUT)

    arrived(out, OUT)

    others = pl.ds(0, (group - 1) * tok)
    for region, kind in (
        (qs, Q_OWN),
        (ks, K_OWN),
        (vs, V_OWN),
        (cqs, CQ),
        (pks, PK_OWN),
        (pvs, PV_OWN),
        (stage, OUT),
    ):
        sent(region.at[others], kind)
    sent(meta_v.at[pl.ds(0, 8 * (group - 1))], META)

    @pl.when(has_prev)
    def _():
        sent(pks.at[others], PK_PREV)
        sent(pvs.at[others], PV_PREV)

    @pl.when(has_next)
    def _():
        sent(enc_prev, ENC)
        sent(ks.at[first_half], K_PREV)
        sent(vs.at[first_half], V_PREV)

    @pl.when(has_next & (off == group - 1))
    def _():
        sent(meta_v.at[pl.ds(0, 8 * group)], META_PREV)


def per_device(
    queries, self_keys, self_values, cross_queries, encoded, neighbour_weight, counts, sources
):
    tok, width = queries.shape
    depth = encoded.shape[1]
    group = width // HEAD_DIM
    assert group == REACH
    chunks = lax.axis_size("ctx") // group
    window = group * tok
    span_count = counts.shape[0]
    meta = jnp.concatenate([counts[:, None], sources], axis=1).reshape(1, -1)
    meta = jnp.pad(meta, ((0, 7), (0, HEAD_DIM - meta.shape[1])))
    bf16 = jnp.bfloat16
    anywhere = pl.BlockSpec(memory_space=pl.ANY)
    return pl.pallas_call(
        functools.partial(kernel, group, chunks, span_count),
        out_shape=jax.ShapeDtypeStruct((tok, width), bf16),
        in_specs=[anywhere] * 7,
        out_specs=anywhere,
        scratch_shapes=[
            pltpu.VMEM((window, HEAD_DIM), bf16),
            pltpu.VMEM((2 * window, HEAD_DIM), bf16),
            pltpu.VMEM((2 * window, HEAD_DIM), bf16),
            pltpu.VMEM((window, HEAD_DIM), bf16),
            pltpu.VMEM((8 * (group + 1), HEAD_DIM), jnp.int32),
            pltpu.SMEM((8 * (group + 1), HEAD_DIM), jnp.int32),
            pltpu.VMEM((tok, depth), bf16),
            pltpu.VMEM((tok, depth), bf16),
            pltpu.VMEM((depth, 2 * width), bf16),
            pltpu.VMEM((tok, 2 * width), bf16),
            pltpu.VMEM((tok, 2 * width), bf16),
            pltpu.VMEM((2 * window, HEAD_DIM), bf16),
            pltpu.VMEM((2 * window, HEAD_DIM), bf16),
            pltpu.VMEM((window, HEAD_DIM), jnp.float32),
            pltpu.VMEM((window, HEAD_DIM), bf16),
            pltpu.SemaphoreType.DMA((KINDS,)),
            pltpu.SemaphoreType.DMA((KINDS,)),
            pltpu.SemaphoreType.DMA((LOCALS,)),
        ],
        compiler_params=pltpu.CompilerParams(
            collective_id=0, has_side_effects=True, vmem_limit_bytes=48 * 2**20
        ),
        cost_estimate=pl.CostEstimate(
            flops=4 * window * (window + 2 * tok) * HEAD_DIM,
            bytes_accessed=8 * window * HEAD_DIM * 2,
            transcendentals=window * window,
        ),
    )(queries, self_keys, self_values, cross_queries, encoded, neighbour_weight, meta)


def solution(mesh):
    return jax.shard_map(
        per_device,
        mesh=mesh,
        in_specs=(
            P(("groups", "ctx"), None),
            P(("groups", "ctx"), None),
            P(("groups", "ctx"), None),
            P(("groups", "ctx"), None),
            P(("groups", "ctx"), None),
            P(),
            P(("groups", "ctx")),
            P(("groups", "ctx"), None),
        ),
        out_specs=P(("groups", "ctx"), None),
        check_vma=False,
    )
```

```python
import functools

import jax
import jax.numpy as jnp
from jax import lax
from jax.experimental import pallas as pl
from jax.experimental.pallas import tpu as pltpu
from jax.sharding import PartitionSpec as P

HEAD_DIM = 128
SPAN = 64
REACH = 16
MASKED_SCORE = -1e30
LOG2E = 1.4426950408889634

ENC, Q_OWN, K_OWN, V_OWN, K_PREV, V_PREV, CQ, META, META_PREV = range(9)
PK_OWN, PV_OWN, PK_PREV, PV_PREV, OUT, ENC_PAIR, ENC_PREV_PAIR, KINDS = range(9, 17)
LOCAL_WK, LOCAL_WV, LOCAL_E, LOCAL_META, LOCALS = range(5)


def dot_t(a, b):
    return lax.dot_general(a, b, (((1,), (1,)), ((), ())), preferred_element_type=jnp.float32)


def kernel(
    group,
    chunks,
    span_count,
    q_in,
    k_in,
    v_in,
    cq_in,
    e_in,
    w_in,
    meta_in,
    out,
    qs,
    ks,
    vs,
    cqs,
    meta_v,
    meta_s,
    enc_own,
    enc_prev,
    weight,
    proj_own,
    proj_prev,
    pks,
    pvs,
    self_out,
    stage,
    send,
    recv,
    local,
):
    tok = q_in.shape[0]
    width = q_in.shape[1]
    window = group * tok
    me = lax.axis_index("ctx")
    chunk = lax.div(me, group)
    off = lax.rem(me, group)
    scale = LOG2E * HEAD_DIM ** (-0.5)
    has_prev = chunk > 0
    has_next = chunk < chunks - 1

    def own_peer(step):
        return lax.rem(off + step, group)

    def columns(index):
        return pl.ds(pl.multiple_of(index * HEAD_DIM, HEAD_DIM), HEAD_DIM)

    def rows(index, base=0):
        return pl.ds(pl.multiple_of(base + index * tok, tok), tok)

    def remote(src, dst, kind, device):
        pltpu.make_async_remote_copy(
            src_ref=src,
            dst_ref=dst,
            send_sem=send.at[kind],
            recv_sem=recv.at[kind],
            device_id={"ctx": device},
            device_id_type=pl.DeviceIdType.MESH,
        ).start()

    def arrived(region, kind):
        pltpu.make_async_copy(region, region, recv.at[kind]).wait()

    def sent(region, kind):
        pltpu.make_async_copy(region, region, send.at[kind]).wait()

    half_heads = group // 2
    half_width = width // 2
    half = lax.div(off, half_heads)
    partner = lax.rem(off + half_heads, group)
    first_rows = pl.ds(0, tok)
    pair_rows = pl.ds(tok, tok)
    load_w = [
        pltpu.make_async_copy(
            w_in.at[:, pl.ds(pl.multiple_of(part * width + half * half_width, half_width), half_width)],
            weight.at[:, pl.ds(part * half_width, half_width)],
            local.at[LOCAL_WK + part],
        )
        for part in range(2)
    ]
    load_e = pltpu.make_async_copy(e_in, enc_own.at[first_rows], local.at[LOCAL_E])
    load_e.start()
    load_w[0].start()
    load_w[1].start()

    barrier = pltpu.get_barrier_semaphore()

    def greet(device):
        pl.semaphore_signal(
            barrier, inc=1, device_id={"ctx": device}, device_id_type=pl.DeviceIdType.MESH
        )

    @pl.loop(1, group)
    def _(step):
        greet(chunk * group + own_peer(step))

    @pl.when(has_prev)
    def _():
        @pl.loop(0, group)
        def _(step):
            greet((chunk - 1) * group + own_peer(step))

    @pl.when(has_next)
    def _():
        @pl.loop(0, group)
        def _(step):
            greet((chunk + 1) * group + own_peer(step))

    friends = group - 1 + jnp.where(has_prev, group, 0) + jnp.where(has_next, group, 0)
    pl.semaphore_wait(barrier, friends)

    @pl.when(has_next)
    def _():
        remote(e_in, enc_prev.at[first_rows], ENC, (chunk + 1) * group + off)

    remote(e_in, enc_own.at[pair_rows], ENC_PAIR, chunk * group + partner)

    def send_next(step):
        peer = own_peer(step)
        cols = columns(peer)

        @pl.when(has_next)
        def _():
            target = (chunk + 1) * group + peer
            remote(k_in.at[:, cols], ks.at[rows(off)], K_PREV, target)
            remote(v_in.at[:, cols], vs.at[rows(off)], V_PREV, target)

    early = group // 2

    @pl.loop(0, group)
    def _(step):
        peer = own_peer(step)
        cols = columns(peer)

        @pl.when(step % 2 == 0)
        def _():
            send_next(lax.div(step, 2))

        @pl.when(step > 0)
        def _():
            target = chunk * group + peer
            remote(k_in.at[:, cols], ks.at[rows(off, window)], K_OWN, target)
            remote(v_in.at[:, cols], vs.at[rows(off, window)], V_OWN, target)
            remote(q_in.at[:, cols], qs.at[rows(off)], Q_OWN, target)

    def own_copy(src, dst, kind):
        pltpu.make_async_copy(src, dst, recv.at[kind]).start()

    mine = columns(off)
    own_copy(k_in.at[:, mine], ks.at[rows(off, window)], K_OWN)
    own_copy(v_in.at[:, mine], vs.at[rows(off, window)], V_OWN)
    own_copy(q_in.at[:, mine], qs.at[rows(off)], Q_OWN)
    own_copy(cq_in.at[:, mine], cqs.at[rows(off)], CQ)
    own_meta = pl.ds(pl.multiple_of(8 * (off + 1), 8), 8)
    own_copy(meta_in, meta_v.at[own_meta], META)

    @pl.when(has_next & (off == group - 1))
    def _():
        @pl.loop(0, group)
        def _(step):
            remote(meta_in, meta_v.at[pl.ds(0, 8)], META_PREV, (chunk + 1) * group + own_peer(step))

    @pl.loop(1, group)
    def _(step):
        peer = own_peer(step)
        target = chunk * group + peer
        remote(cq_in.at[:, columns(peer)], cqs.at[rows(off)], CQ, target)
        remote(meta_in, meta_v.at[own_meta], META, target)

    load_w[0].wait()
    load_w[1].wait()
    load_e.wait()

    def project(encoded, proj, base, key_kind, value_kind, also):
        @pl.loop(0, half_heads // 2)
        def _(step):
            pair = lax.rem(lax.div(off, 2) + step, half_heads // 2)
            for part, (dst, kind) in enumerate(((pks, key_kind), (pvs, value_kind))):
                start = pl.multiple_of(part * half_width + pair * 2 * HEAD_DIM, 2 * HEAD_DIM)
                both = pl.ds(start, 2 * HEAD_DIM)
                proj[:, both] = jnp.dot(
                    encoded[...], weight[:, both], preferred_element_type=jnp.float32
                ).astype(jnp.bfloat16)
                for side in range(2):
                    peer = half * half_heads + pair * 2 + side
                    start = part * half_width + (pair * 2 + side) * HEAD_DIM
                    cols = pl.ds(pl.multiple_of(start, HEAD_DIM), HEAD_DIM)
                    for source, owner in ((first_rows, off), (pair_rows, partner)):
                        goal = dst.at[rows(owner, base)]

                        @pl.when(peer != off)
                        def _():
                            remote(proj.at[source, cols], goal, kind, chunk * group + peer)

                        @pl.when(peer == off)
                        def _():
                            own_copy(proj.at[source, cols], goal, kind)

            also(step)

    def send_two(step):
        send_next(early + 2 * step)
        send_next(early + 2 * step + 1)

    arrived(enc_own.at[pair_rows], ENC_PAIR)
    project(enc_own, proj_own, window, PK_OWN, PV_OWN, send_two)

    @pl.when(has_prev)
    def _():
        arrived(enc_prev.at[first_rows], ENC)
        remote(enc_prev.at[first_rows], enc_prev.at[pair_rows], ENC_PREV_PAIR, chunk * group + partner)
        arrived(enc_prev.at[pair_rows], ENC_PREV_PAIR)
        project(enc_prev, proj_prev, 0, PK_PREV, PV_PREV, lambda step: None)

    first_half = pl.ds(0, window)
    second_half = pl.ds(window, window)

    @pl.when(jnp.logical_not(has_prev))
    def _():
        ks[first_half, :] = jnp.zeros((window, HEAD_DIM), jnp.bfloat16)
        vs[first_half, :] = jnp.zeros((window, HEAD_DIM), jnp.bfloat16)
        pks[first_half, :] = jnp.zeros((window, HEAD_DIM), jnp.bfloat16)
        pvs[first_half, :] = jnp.zeros((window, HEAD_DIM), jnp.bfloat16)
        meta_v[pl.ds(0, 8), :] = jnp.zeros((8, meta_v.shape[1]), jnp.int32)

    arrived(qs, Q_OWN)
    arrived(ks.at[second_half], K_OWN)
    arrived(vs.at[second_half], V_OWN)

    @pl.when(has_prev)
    def _():
        arrived(ks.at[first_half], K_PREV)
        arrived(vs.at[first_half], V_PREV)

    tile = 2 * tok
    reach = window + tile

    @pl.loop(0, window // tile)
    def _(index):
        start = pl.multiple_of(index * tile, tile)
        queries = qs[pl.ds(start, tile), :]
        keys = ks[pl.ds(start, reach), :]
        values = vs[pl.ds(start, reach), :]
        least = jnp.where(has_prev, 0, window - start)
        scores = dot_t(queries, keys)
        row = lax.broadcasted_iota(jnp.int32, (tile, tile), 0)
        col = lax.broadcasted_iota(jnp.int32, (tile, tile), 1)
        mid = lax.broadcasted_iota(jnp.int32, (1, window - tile), 1) + tile
        head = jnp.where((col > row) & (col >= least), scores[:, :tile], MASKED_SCORE)
        body = jnp.where(mid >= least, scores[:, tile:window], MASKED_SCORE)
        tail = jnp.where(col <= row, scores[:, window:], MASKED_SCORE)
        scores = jnp.concatenate([head, body, tail], axis=1)
        largest = jnp.max(scores, axis=-1, keepdims=True)
        exponent = jnp.exp2((scores - largest) * scale)
        total = jnp.sum(exponent, axis=-1, keepdims=True)
        result = jnp.dot(exponent.astype(jnp.bfloat16), values, preferred_element_type=jnp.float32)
        self_out[pl.ds(start, tile), :] = result / total

    arrived(meta_v.at[pl.ds(8, 8 * group)], META)
    arrived(cqs, CQ)
    arrived(pks.at[second_half], PK_OWN)
    arrived(pvs.at[second_half], PV_OWN)

    @pl.when(has_prev)
    def _():
        arrived(meta_v.at[pl.ds(0, 8)], META_PREV)
        arrived(pks.at[first_half], PK_PREV)
        arrived(pvs.at[first_half], PV_PREV)

    to_scalar = pltpu.make_async_copy(meta_v, meta_s, local.at[LOCAL_META])
    to_scalar.start()
    to_scalar.wait()

    @pl.loop(0, window // tile)
    def _(index):
        start = pl.multiple_of(index * tile, tile)
        lowest = pl.multiple_of(start + SPAN, SPAN)
        across = window + tile - 2 * SPAN
        keys = pks[pl.ds(lowest, across), :]
        values = pvs[pl.ds(lowest, across), :]
        scores = dot_t(cqs[pl.ds(start, tile), :], keys)
        place = lax.broadcasted_iota(jnp.int32, (1, across), 1) + lowest
        parts, totals = [], []
        for piece in range(tile // SPAN):
            span = index * (tile // SPAN) + piece
            entry = span + span_count - 1
            block = lax.div(entry, span_count) * 8
            lane = lax.rem(entry, span_count) * 3
            real = has_prev | (span > 0)
            count = jnp.where(real, meta_s[block, lane], 0)
            times = jnp.zeros((1, across), jnp.float32)
            for slot in range(2):
                first = meta_s[block, lane + 1 + slot] * SPAN - (chunk - 1) * window
                first = jnp.where(slot < count, first, -4 * window)
                inside = (place >= first) & (place < first + 2 * SPAN)
                times = times + jnp.where(inside, 1.0, 0.0)
            piece_scores = scores[piece * SPAN : (piece + 1) * SPAN]
            piece_scores = jnp.where(times > 0.0, piece_scores, MASKED_SCORE)
            largest = jnp.max(piece_scores, axis=-1, keepdims=True)
            exponent = jnp.exp2((piece_scores - largest) * scale) * times
            total = jnp.sum(exponent, axis=-1, keepdims=True)
            totals.append(total + jnp.where(count > 0, 0.0, 1.0))
            parts.append(exponent.astype(jnp.bfloat16))
        result = jnp.dot(
            jnp.concatenate(parts, axis=0), values, preferred_element_type=jnp.float32
        ) / jnp.concatenate(totals, axis=0)
        both = self_out[pl.ds(start, tile), :] + result
        stage[pl.ds(start, tile), :] = both.astype(jnp.bfloat16)
        for half in range(tile // tok):
            owner = index * (tile // tok) + half

            @pl.when(owner != off)
            def _():
                remote(stage.at[rows(owner)], out.at[:, mine], OUT, chunk * group + owner)

            @pl.when(owner == off)
            def _():
                own_copy(stage.at[rows(owner)], out.at[:, mine], OUT)

    arrived(out, OUT)

    others = pl.ds(0, (group - 1) * tok)
    for region, kind in (
        (qs, Q_OWN),
        (ks, K_OWN),
        (vs, V_OWN),
        (cqs, CQ),
        (stage, OUT),
    ):
        sent(region.at[others], kind)
    sent(meta_v.at[pl.ds(0, 8 * (group - 1))], META)
    sent(enc_own.at[first_rows], ENC_PAIR)
    projected = pl.ds(0, 2 * (half_heads - 1) * tok)
    sent(pks.at[projected], PK_OWN)
    sent(pvs.at[projected], PV_OWN)

    @pl.when(has_prev)
    def _():
        sent(pks.at[projected], PK_PREV)
        sent(pvs.at[projected], PV_PREV)
        sent(enc_prev.at[first_rows], ENC_PREV_PAIR)

    @pl.when(has_next)
    def _():
        sent(enc_prev.at[first_rows], ENC)
        sent(ks.at[first_half], K_PREV)
        sent(vs.at[first_half], V_PREV)

    @pl.when(has_next & (off == group - 1))
    def _():
        sent(meta_v.at[pl.ds(0, 8 * group)], META_PREV)


def per_device(
    queries, self_keys, self_values, cross_queries, encoded, neighbour_weight, counts, sources
):
    tok, width = queries.shape
    depth = encoded.shape[1]
    group = width // HEAD_DIM
    assert group == REACH
    chunks = lax.axis_size("ctx") // group
    window = group * tok
    span_count = counts.shape[0]
    meta = jnp.concatenate([counts[:, None], sources], axis=1).reshape(1, -1)
    meta = jnp.pad(meta, ((0, 7), (0, HEAD_DIM - meta.shape[1])))
    bf16 = jnp.bfloat16
    anywhere = pl.BlockSpec(memory_space=pltpu.HBM)
    return pl.pallas_call(
        functools.partial(kernel, group, chunks, span_count),
        out_shape=jax.ShapeDtypeStruct((tok, width), bf16),
        in_specs=[anywhere] * 7,
        out_specs=anywhere,
        scratch_shapes=[
            pltpu.VMEM((window, HEAD_DIM), bf16),
            pltpu.VMEM((2 * window, HEAD_DIM), bf16),
            pltpu.VMEM((2 * window, HEAD_DIM), bf16),
            pltpu.VMEM((window, HEAD_DIM), bf16),
            pltpu.VMEM((8 * (group + 1), HEAD_DIM), jnp.int32),
            pltpu.SMEM((8 * (group + 1), HEAD_DIM), jnp.int32),
            pltpu.VMEM((2 * tok, depth), bf16),
            pltpu.VMEM((2 * tok, depth), bf16),
            pltpu.VMEM((depth, width), bf16),
            pltpu.VMEM((2 * tok, width), bf16),
            pltpu.VMEM((2 * tok, width), bf16),
            pltpu.VMEM((2 * window, HEAD_DIM), bf16),
            pltpu.VMEM((2 * window, HEAD_DIM), bf16),
            pltpu.VMEM((window, HEAD_DIM), jnp.float32),
            pltpu.VMEM((window, HEAD_DIM), bf16),
            pltpu.SemaphoreType.DMA((KINDS,)),
            pltpu.SemaphoreType.DMA((KINDS,)),
            pltpu.SemaphoreType.DMA((LOCALS,)),
        ],
        compiler_params=pltpu.CompilerParams(
            collective_id=0, has_side_effects=True, vmem_limit_bytes=63 * 2**20 + 2**19
        ),
        cost_estimate=pl.CostEstimate(
            flops=4 * window * (window + 2 * tok) * HEAD_DIM,
            bytes_accessed=8 * window * HEAD_DIM * 2,
            transcendentals=window * window,
        ),
    )(queries, self_keys, self_values, cross_queries, encoded, neighbour_weight, meta)


def solution(mesh):
    return jax.shard_map(
        per_device,
        mesh=mesh,
        in_specs=(
            P(("groups", "ctx"), None),
            P(("groups", "ctx"), None),
            P(("groups", "ctx"), None),
            P(("groups", "ctx"), None),
            P(("groups", "ctx"), None),
            P(),
            P(("groups", "ctx")),
            P(("groups", "ctx"), None),
        ),
        out_specs=P(("groups", "ctx"), None),
        check_vma=False,
    )
```
